256 devices in a mesh: blk: 128 (over z, x_hi, y, core), rep: 2 (over x_lo).
Axes of the slice: x: 4 (x_hi: 2, x_lo: 2; x = x_hi * 2 + x_lo), y: 4, z: 8, core: 2. Of those that a mesh axis runs over, the one named last changes fastest.
Arguments:
- image: bfloat16 [2, 98304, 1152], P('rep', 'blk'), may hold values from -52 to 52
- text: bfloat16 [2, 98304, 1152], P('rep', 'blk'), may hold values from -52 to 52
- log_temp: float32 [1], replicated, may hold values from 1 to 2
- bias: float32 [1], replicated, may hold values from -4 to -2
Outputs:
- loss: float32 [1], replicated
- grad_image: float32 [2, 98304, 1152], P('rep', 'blk')
- grad_text: float32 [2, 98304, 1152], P('rep', 'blk')
- grad_temp: float32 [1], replicated
- grad_bias: float32 [1], replicated
The draws below stay inside these ranges and needn't reach their ends.
All inputs are finite; a program needn't handle non-finite values.
Results may differ from the reference program's by a relative error of at most 0.0034.
Values may be sent and summed in bfloat16 or wider, within the bound.
No kernel may reach another device: no remote copies, remote signals or barrier semaphores. Data moves between devices by JAX's collectives and lax.ppermute only.
A program may use at most 128 MiB of HBM per device.

```python
import jax
import jax.numpy as jnp
from jax import lax

D = 1152
B = 768
SPANS = 3
ROWS = 98304
REPS = 2


def shared_base(key):
    key_direction, key_noise, key_centre, key_label = jax.random.split(key, 4)
    direction = jax.random.truncated_normal(key_direction, -5.0, 5.0, (REPS, 1, D), jnp.float32)
    noise = jax.random.truncated_normal(key_noise, -5.0, 5.0, (REPS, ROWS, D), jnp.float32)
    centres = jax.random.truncated_normal(key_centre, -5.0, 5.0, (64, D), jnp.float32)
    labels = jax.random.randint(key_label, (REPS, ROWS), 0, 64)
    clustered = jnp.take(centres, labels, axis=0)
    position = jnp.arange(ROWS, dtype=jnp.float32) / ROWS
    odd = (jnp.arange(REPS) % 2).astype(jnp.float32)
    rising = odd[:, None] + (1.0 + 0.5 * odd)[:, None] * position[None, :]
    return noise + 1.2 * clustered + rising[:, :, None] * direction


def draw_image(key, part):
    base = shared_base(key)
    values = base * D ** (-0.5)
    return values.astype(jnp.bfloat16)


def draw_text(key, part):
    base = shared_base(key)
    key = jax.random.fold_in(key, 7)
    key_noise = jax.random.fold_in(key, 0)
    extra = jax.random.truncated_normal(key_noise, -5.0, 5.0, (REPS, ROWS, D), jnp.float32)
    values = (0.8 * base + 0.6 * extra) * D ** (-0.5)
    return values.astype(jnp.bfloat16)


def setup_inputs(seed: int = 0) -> dict:
    keys = jax.random.split(jax.random.key(seed), 5)
    return {
        "image": draw_image(jax.random.fold_in(keys[4], 71), 0),
        "text": draw_text(jax.random.fold_in(keys[4], 71), 0),
        "log_temp": jnp.clip(jax.random.uniform(keys[2], (1,), jnp.float32, 1.0, 2.0), 1.0, 2.0),
        "bias": jnp.clip(jax.random.uniform(keys[3], (1,), jnp.float32, -4.0, -2.0), -4.0, -2.0),
    }


def unit_rows(raw):
    scale = lax.rsqrt(lax.optimization_barrier(jnp.sum(raw * raw, axis=-1, keepdims=True)) + 1e-06)
    return (raw * scale, scale)

def unit_back(grad, normed, scale):
    return (grad - normed * lax.optimization_barrier(jnp.sum(normed * grad, axis=-1, keepdims=True))) * scale

def pair_block(left, right, temper, offset_bias, positive):
    raw = lax.dot_general(left, right, (((1,), (1,)), ((), ())), preferred_element_type=jnp.float32)
    logits = temper * raw + offset_bias
    rows = left.shape[0]
    diagonal = lax.broadcasted_iota(jnp.int32, (rows, rows), 0) == lax.broadcasted_iota(jnp.int32, (rows, rows), 1)
    sign = jnp.where(jnp.logical_and(diagonal, positive), 1.0, -1.0).astype(jnp.float32)
    margin = sign * logits
    total = jnp.sum(jnp.logaddexp(0.0, -margin))
    slope = -sign * jax.nn.sigmoid(-margin)
    return (total, jnp.sum(slope * temper * raw), jnp.sum(slope), slope.astype(jnp.bfloat16))

def reference(image, text, log_temp, bias):
    temper = jnp.exp(log_temp[0])
    offset_bias = bias[0]
    blocks = ROWS // B
    image_grads = []
    text_grads = []
    sums = (jnp.zeros((), jnp.float32), jnp.zeros((), jnp.float32), jnp.zeros((), jnp.float32))
    for group in range(REPS):
        unit_image, image_scale = unit_rows(image[group].astype(jnp.float32))
        unit_text, text_scale = unit_rows(text[group].astype(jnp.float32))
        image_blocks = unit_image.astype(jnp.bfloat16).reshape(blocks, B, D)
        text_blocks = unit_text.astype(jnp.bfloat16).reshape(blocks, B, D)

        def visit(carry, index):
            grad_store, loss_sum, temp_sum, bias_sum = carry
            left = lax.dynamic_index_in_dim(image_blocks, index, 0, keepdims=False)
            grad_left = jnp.zeros((B, D), jnp.float32)
            for offset in range(SPANS):
                source = ((index - offset) % blocks).astype(jnp.int32)
                right = lax.dynamic_index_in_dim(text_blocks, source, 0, keepdims=False)
                total, dtemp, dbias, slope_low = pair_block(left, right, temper, offset_bias, offset == 0)
                grad_left = grad_left + temper * jnp.dot(slope_low, right, preferred_element_type=jnp.float32)
                term = temper * lax.dot_general(slope_low, left, (((0,), (0,)), ((), ())), preferred_element_type=jnp.float32)
                current = lax.dynamic_index_in_dim(grad_store, source, 0, keepdims=False)
                grad_store = lax.dynamic_update_index_in_dim(grad_store, current + term, source, 0)
                loss_sum = loss_sum + total
                temp_sum = temp_sum + dtemp
                bias_sum = bias_sum + dbias
            return ((grad_store, loss_sum, temp_sum, bias_sum), grad_left)
        start = (jnp.zeros((blocks, B, D), jnp.float32),) + sums
        final, grad_lefts = lax.scan(visit, start, jnp.arange(blocks, dtype=jnp.int32))
        sums = final[1:]
        image_grads.append(unit_back(grad_lefts.reshape(ROWS, D), unit_image, image_scale))
        text_grads.append(unit_back(final[0].reshape(ROWS, D), unit_text, text_scale))
    pairs = float(REPS * ROWS * SPANS * B)
    loss = (sums[0] / pairs).reshape(1)
    grad_temp = (sums[1] / pairs).reshape(1)
    grad_bias = (sums[2] / pairs).reshape(1)
    return (loss, jnp.stack(image_grads), jnp.stack(text_grads), grad_temp, grad_bias)
```

```python
import functools

import jax
import jax.numpy as jnp
from jax import lax
from jax.experimental import pallas as pl
from jax.experimental.pallas import tpu as pltpu
from jax.sharding import PartitionSpec as P

SPANS = 3
TILE = 256
LOW = jnp.bfloat16
F32 = jnp.float32
VMEM_LIMIT = 16 * 1024 * 1024


def params():
    return pltpu.CompilerParams(vmem_limit_bytes=VMEM_LIMIT)


def cost(flops, moved, trans=0):
    return pl.CostEstimate(flops=0, bytes_accessed=0, transcendentals=0)


def smem():
    return pl.BlockSpec(memory_space=pltpu.SMEM)


def vmem():
    return pl.BlockSpec(memory_space=pltpu.VMEM)


def hbm():
    return pl.BlockSpec(memory_space=pltpu.HBM)


def near(*values):
    return [pltpu.with_memory_space_constraint(v, pltpu.VMEM) for v in values]


def far(*values):
    return [pltpu.with_memory_space_constraint(v, pltpu.HBM) for v in values]


def unit_rows(raw):
    scale = lax.rsqrt(jnp.sum(raw * raw, axis=-1, keepdims=True) + 1e-06)
    return raw * scale, scale


def dot_t(x, y):
    return lax.dot_general(x, y, (((1,), (1,)), ((), ())), preferred_element_type=F32)


def dot(x, y):
    return jnp.dot(x, y, preferred_element_type=F32)


def pieces(rows):
    return [slice(r, r + TILE) for r in range(0, rows, TILE)]


def fold(values):
    rows, width = values.shape
    part = jnp.sum(values.reshape(rows // 8, 8, width), axis=0)
    return functools.reduce(jnp.add, [part[:, c : c + 128] for c in range(0, width, 128)])


def joined(p, q):
    return p + q + p * q


def log_fold(grown):
    rows, width = grown.shape
    groups = grown.reshape(rows // 64, 8, 8, width)
    parts = [groups[:, i] for i in range(8)]
    while len(parts) > 1:
        parts = [joined(p, q) for p, q in zip(parts[::2], parts[1::2])]
    return fold(jnp.log1p(parts[0]).reshape(rows // 8, width))


def share(grown):
    whole = 1.0 + grown
    inverse = pl.reciprocal(whole, approx=True)
    inverse = inverse * (2.0 - whole * inverse)
    return grown * inverse


def sums_of(grown, slope, raw):
    return log_fold(grown), fold(slope * raw), fold(slope)


def put_sums(sums_in, sums_ref, total, weight):
    for k in range(3):
        rows = slice(8 * k, 8 * k + 8)
        sums_ref[rows, :] = (sums_in[rows, :] if sums_in is not None else 0.0) + weight * total[k]


def unit_kernel(even_ref, image_ref, text_ref, a_ref, b_ref, slots, sems):
    even = even_ref[0] == 1
    parts = pieces(a_ref.shape[0])

    @pl.when(even)
    def _():
        for k, ref in enumerate((image_ref, text_ref)):
            for c, rows in enumerate(parts):
                pltpu.make_async_copy(ref.at[0, rows], slots.at[k, c], sems.at[k, c]).start()

    @pl.when(jnp.logical_not(even))
    def _():
        for k, ref in enumerate((text_ref, image_ref)):
            for c, rows in enumerate(parts):
                pltpu.make_async_copy(ref.at[0, rows], slots.at[k, c], sems.at[k, c]).start()

    for k, out_ref in enumerate((a_ref, b_ref)):
        for c, rows in enumerate(parts):
            pltpu.make_async_copy(image_ref.at[0, rows], slots.at[k, c], sems.at[k, c]).wait()
            out_ref[rows, :] = unit_rows(slots[k, c].astype(F32))[0].astype(LOW)


def unit_blocks(even, image, text):
    _, rows, width = image.shape
    full = pltpu.VMEM((rows, width), LOW)
    count = rows // TILE
    return pl.pallas_call(
        unit_kernel,
        in_specs=[smem(), hbm(), hbm()],
        out_specs=[vmem()] * 2,
        out_shape=[full] * 2,
        scratch_shapes=[
            pltpu.VMEM((2, count, TILE, width), LOW),
            pltpu.SemaphoreType.DMA((2, count)),
        ],
        compiler_params=params(),
        cost_estimate=cost(rows * width * 8, rows * width * 12),
        name="unit_blocks",
    )(even, *far(image, text))


def own_kernel(scalar_ref, a_ref, b_ref, slope_ref, sums_ref):
    temper, bias = scalar_ref[0], scalar_ref[1]
    total = None
    for rows in pieces(a_ref.shape[0]):
        raw = dot_t(a_ref[rows, :], b_ref[...])
        logits = temper * raw + bias
        row = lax.broadcasted_iota(jnp.int32, raw.shape, 0) + rows.start
        diagonal = row == lax.broadcasted_iota(jnp.int32, raw.shape, 1)
        grown = jnp.exp(jnp.where(diagonal, -logits, logits))
        part = share(grown)
        slope = jnp.where(diagonal, -part, part)
        slope_ref[rows, :] = slope.astype(LOW)
        part = sums_of(grown, slope, raw)
        total = part if total is None else [p + q for p, q in zip(total, part)]
    put_sums(None, sums_ref, total, 1.0)


def own_slopes(scalars, a, b):
    rows, width = a.shape
    return pl.pallas_call(
        own_kernel,
        in_specs=[smem(), vmem(), vmem()],
        out_specs=[vmem(), vmem()],
        out_shape=[pltpu.VMEM((rows, rows), LOW), pltpu.VMEM((24, 128), F32)],
        compiler_params=params(),
        cost_estimate=cost(2 * rows * rows * width, rows * width * 6, 3 * rows * rows),
        name="own_slopes",
    )(scalars, *near(a, b))


def pair_slopes(temper, bias, x, y):
    raw = dot_t(x, y)
    grown = jnp.exp(temper * raw + bias)
    return raw, grown, share(grown)


def slopes_kernel(scalar_ref, x_ref, y_ref, sums_in, slope_ref, sums_ref, *, weight):
    total = None
    for rows in pieces(x_ref.shape[0]):
        raw, grown, slope = pair_slopes(scalar_ref[0], scalar_ref[1], x_ref[rows, :], y_ref[...])
        slope_ref[rows, :] = slope.astype(LOW)
        part = sums_of(grown, slope, raw)
        total = part if total is None else [p + q for p, q in zip(total, part)]
    put_sums(sums_in, sums_ref, total, weight)


def slopes(scalars, x, y, sums, weight):
    rows, width = x.shape
    other = y.shape[0]
    return pl.pallas_call(
        functools.partial(slopes_kernel, weight=weight),
        in_specs=[smem(), vmem(), vmem(), vmem()],
        out_specs=[vmem(), vmem()],
        out_shape=[pltpu.VMEM((rows, other), LOW), pltpu.VMEM((24, 128), F32)],
        compiler_params=params(),
        cost_estimate=cost(2 * rows * other * width, (rows + other) * width * 4, 3 * rows * other),
        name="slopes",
    )(scalars, *near(x, y, sums))


def late_kernel(even_ref, scalar_ref, x_ref, y_ref, w_ref, sums_in, slope_ref, sums_ref):
    temper, bias = scalar_ref[0], scalar_ref[1]
    total = None
    for rows in pieces(x_ref.shape[0]):
        raw, grown, slope = pair_slopes(temper, bias, x_ref[rows, :], y_ref[...])
        slope_ref[rows, :] = slope.astype(LOW)
        part = sums_of(grown, slope, raw)
        total = part if total is None else [p + q for p, q in zip(total, part)]
    put_sums(sums_in, sums_ref, total, 1.0)
    half = x_ref.shape[0] // 2

    def rest(left, right):
        raw, grown, slope = pair_slopes(temper, bias, left, right)
        put_sums(sums_ref, sums_ref, sums_of(grown, slope, raw), 1.0)

    @pl.when(even_ref[0] == 1)
    def _():
        rest(w_ref[...], y_ref[half:, :])

    @pl.when(even_ref[0] == 0)
    def _():
        rest(y_ref[...], w_ref[:half, :])


def late_slopes(even, scalars, x, y, w, sums):
    rows, width = x.shape
    return pl.pallas_call(
        late_kernel,
        in_specs=[smem(), smem()] + [vmem()] * 4,
        out_specs=[vmem(), vmem()],
        out_shape=[pltpu.VMEM((rows, rows), LOW), pltpu.VMEM((24, 128), F32)],
        compiler_params=params(),
        cost_estimate=cost(3 * rows * rows * width, rows * width * 8, 4 * rows * rows),
        name="late_slopes",
    )(even, scalars, *near(x, y, w, sums))


def start_kernel(own_ref, a_ref, b_ref, other_ref, e_ref, ga_ref, gb_ref):
    for rows in pieces(a_ref.shape[0]):
        ga_ref[rows, :] = dot(own_ref[rows, :], b_ref[...])
        term = lax.dot_general(
            own_ref[:, rows], a_ref[...], (((0,), (0,)), ((), ())), preferred_element_type=F32
        )
        gb_ref[rows, :] = term + dot(other_ref[rows, :], e_ref[...])


def start_grads(own, a, b, other, e):
    rows, width = a.shape
    grad = pltpu.VMEM((rows, width), F32)
    return pl.pallas_call(
        start_kernel,
        in_specs=[vmem()] * 5,
        out_specs=[vmem()] * 2,
        out_shape=[grad, grad],
        compiler_params=params(),
        cost_estimate=cost(6 * rows * rows * width, rows * width * 16),
        name="start_grads",
    )(*near(own, a, b, other, e))


def back(grad, raw):
    unit, scale = unit_rows(raw.astype(F32))
    return (grad - unit * jnp.sum(unit * grad, axis=-1, keepdims=True)) * scale


def start_raw(first, even_in, odd_in, slots, sems, parts):
    @pl.when(first)
    def _():
        for c, rows in enumerate(parts):
            pltpu.make_async_copy(even_in.at[0, rows], slots.at[c], sems.at[0, c]).start()

    @pl.when(jnp.logical_not(first))
    def _():
        for c, rows in enumerate(parts):
            pltpu.make_async_copy(odd_in.at[0, rows], slots.at[c], sems.at[0, c]).start()


def start_out(first, c, rows, even_out, odd_out, slots, sems):
    @pl.when(first)
    def _():
        pltpu.make_async_copy(slots.at[c], even_out.at[0, rows], sems.at[1, c]).start()

    @pl.when(jnp.logical_not(first))
    def _():
        pltpu.make_async_copy(slots.at[c], odd_out.at[0, rows], sems.at[1, c]).start()


def b_kernel(
    even_ref, scalar_ref, image_ref, text_ref, s_ref, p_ref, g_ref,
    image_out, text_out, raws, slots, sems,
):
    even = even_ref[0] == 1
    parts = pieces(g_ref.shape[0])
    start_raw(even, text_ref, image_ref, raws, sems, parts)
    for c, rows in enumerate(parts):
        total = g_ref[rows, :] + dot(s_ref[rows, :], p_ref[...])
        pltpu.make_async_copy(text_ref.at[0, rows], raws.at[c], sems.at[0, c]).wait()
        slots[c] = back(scalar_ref[0] * total, raws[c])
        start_out(even, c, rows, text_out, image_out, slots, sems)
    for c, rows in enumerate(parts):
        pltpu.make_async_copy(slots.at[c], text_out.at[0, rows], sems.at[1, c]).wait()


def finish_b(even, scalars, image, text, s, p, grad):
    rows, width = grad.shape
    out = pltpu.HBM((1, rows, width), F32)
    count = rows // TILE
    return pl.pallas_call(
        b_kernel,
        in_specs=[smem(), smem(), hbm(), hbm()] + [vmem()] * 3,
        out_specs=[hbm()] * 2,
        out_shape=[out, out],
        scratch_shapes=[
            pltpu.VMEM((count, TILE, width), LOW),
            pltpu.VMEM((count, TILE, width), F32),
            pltpu.SemaphoreType.DMA((2, count)),
        ],
        compiler_params=params(),
        cost_estimate=cost(2 * rows * rows * width, rows * width * 14),
        name="finish_b",
    )(even, scalars, *far(image, text), *near(s, p, grad))


def a_kernel(
    even_ref, scalar_ref, image_ref, text_ref, a_ref, f_ref, q_ref, g_ref, _image, _text,
    image_out, text_out, raws, slots, sems,
):
    even = even_ref[0] == 1
    temper, bias = scalar_ref[0], scalar_ref[1]
    parts = pieces(g_ref.shape[0])
    start_raw(even, image_ref, text_ref, raws, sems, parts)
    for c, rows in enumerate(parts):
        total = g_ref[rows, :]
        for y_ref in (f_ref, q_ref):
            slope = pair_slopes(temper, bias, a_ref[rows, :], y_ref[...])[2]
            total = total + dot(slope.astype(LOW), y_ref[...])
        pltpu.make_async_copy(image_ref.at[0, rows], raws.at[c], sems.at[0, c]).wait()
        slots[c] = back(temper * total, raws[c])
        start_out(even, c, rows, image_out, text_out, slots, sems)
    for c, rows in enumerate(parts):
        pltpu.make_async_copy(slots.at[c], image_out.at[0, rows], sems.at[1, c]).wait()


def finish_a(even, scalars, image, text, a, f, q, grad, image_out, text_out):
    rows, width = grad.shape
    out = pltpu.HBM((1, rows, width), F32)
    count = rows // TILE
    return pl.pallas_call(
        a_kernel,
        in_specs=[smem(), smem(), hbm(), hbm()] + [vmem()] * 4 + [hbm()] * 2,
        out_specs=[hbm()] * 2,
        out_shape=[out, out],
        input_output_aliases={8: 0, 9: 1},
        scratch_shapes=[
            pltpu.VMEM((count, TILE, width), LOW),
            pltpu.VMEM((count, TILE, width), F32),
            pltpu.SemaphoreType.DMA((2, count)),
        ],
        compiler_params=params(),
        cost_estimate=cost(8 * rows * rows * width, rows * width * 20),
        name="finish_a",
    )(even, scalars, *far(image, text), *near(a, f, q, grad), *far(image_out, text_out))


def partner(block):
    count = lax.axis_size("blk")
    return lax.ppermute(block, "blk", [(i, i ^ 1) for i in range(count)])


def outward(block):
    count = lax.axis_size("blk")
    return lax.ppermute(block, "blk", [(i, (i + (2 if i % 2 else -2)) % count) for i in range(count)])


def inward(block):
    count = lax.axis_size("blk")
    return lax.ppermute(block, "blk", [(i, (i + (1 if i % 2 else -1)) % count) for i in range(count)])


def swap(sums, mask):
    total = lax.axis_size("blk") * lax.axis_size("rep")
    route = [(i, i ^ mask) for i in range(total)]
    return sums + lax.ppermute(sums, ("blk", "rep"), route)


def after(value, *others):
    return lax.optimization_barrier((value, *others))[0]


def body(image, text, log_temp, bias):
    _, rows, width = image.shape
    temper = jnp.exp(log_temp)
    scalars = jnp.concatenate([temper, bias])
    even = (lax.rem(lax.axis_index("blk"), 2) == 0).astype(jnp.int32).reshape(1)

    a, b = unit_blocks(even, image, text)
    p = outward(a)
    e = partner(b)
    w = partner(a)

    s_own, sums = own_slopes(scalars, a, b)
    q = inward(e)
    s_e, sums = slopes(scalars, b, e, sums, 0.5)
    grad_a, grad_b = start_grads(after(s_own, sums), a, b, s_e, e)
    s_p, sums = late_slopes(even, scalars, b, after(p, grad_b), w, sums)
    f = partner(after(p, sums))
    small = jnp.sum(sums.reshape(3, 8, 128), axis=1)
    for mask in (2, 128, 64):
        small = swap(small, mask)
    small = after(small, q)
    total = swap(small, 16)
    image_out, text_out = finish_b(
        after(even, small), scalars, image, text, s_p, p, grad_b
    )
    small = after(total, image_out)
    for mask in (32,):
        small = swap(small, mask)
    total = swap(small, 8)
    grad_image, grad_text = finish_a(
        after(even, small), scalars, image, text, a, f, q, grad_a, image_out, text_out
    )
    small = after(total, grad_image)
    for mask in (4, 1):
        small = swap(small, mask)

    pairs = float(lax.axis_size("rep") * lax.axis_size("blk") * rows * SPANS * rows)
    small = jnp.sum(small, axis=1) / pairs
    return (small[0:1], grad_image, grad_text, small[1:2] * temper, small[2:3])


def solution(mesh):
    return jax.shard_map(
        body,
        mesh=mesh,
        in_specs=(P("rep", "blk", None), P("rep", "blk", None), P(), P()),
        out_specs=(P(), P("rep", "blk", None), P("rep", "blk", None), P(), P()),
        check_vma=False,
    )
```

```python
import functools

import jax
import jax.numpy as jnp
from jax import lax
from jax.experimental import pallas as pl
from jax.experimental.pallas import tpu as pltpu
from jax.sharding import PartitionSpec as P

SPANS = 3
TILE = 256
LOW = jnp.bfloat16
F32 = jnp.float32
MASKS = (32, 1, 4, 128, 64, 16, 8)
Q_TURN, F_TURN = 1, 2
A_TURNS = {3: (0, 1), 4: (2,)}


def params(mib=4):
    return pltpu.CompilerParams(vmem_limit_bytes=mib * 1024 * 1024)


def cost(flops, moved, trans=0):
    return pl.CostEstimate(flops=0, bytes_accessed=0, transcendentals=0)


def smem():
    return pl.BlockSpec(memory_space=pltpu.SMEM)


def vmem():
    return pl.BlockSpec(memory_space=pltpu.VMEM)


def hbm():
    return pl.BlockSpec(memory_space=pltpu.HBM)


def near(*values):
    return [pltpu.with_memory_space_constraint(v, pltpu.VMEM) for v in values]


def far(*values):
    return [pltpu.with_memory_space_constraint(v, pltpu.HBM) for v in values]


def unit_rows(raw):
    scale = lax.rsqrt(jnp.sum(raw * raw, axis=-1, keepdims=True) + 1e-06)
    return raw * scale, scale


def dot_t(x, y):
    return lax.dot_general(x, y, (((1,), (1,)), ((), ())), preferred_element_type=F32)


def dot(x, y):
    return jnp.dot(x, y, preferred_element_type=F32)


def pieces(rows, size=TILE):
    return [slice(r, r + size) for r in range(0, rows, size)]


def fold(values):
    rows, width = values.shape
    part = jnp.sum(values.reshape(rows // 8, 8, width), axis=0)
    return functools.reduce(jnp.add, [part[:, c : c + 128] for c in range(0, width, 128)])


def joined(p, q):
    return p + q + p * q


def log_fold(grown):
    rows, width = grown.shape
    groups = grown.reshape(rows // 64, 8, 8, width)
    parts = [groups[:, i] for i in range(8)]
    while len(parts) > 1:
        parts = [joined(p, q) for p, q in zip(parts[::2], parts[1::2])]
    return fold(jnp.log1p(parts[0]).reshape(rows // 8, width))


def share(grown):
    whole = 1.0 + grown
    inverse = pl.reciprocal(whole, approx=True)
    inverse = inverse * (2.0 - whole * inverse)
    return grown * inverse


def sums_of(grown, slope, raw):
    return log_fold(grown), fold(slope * raw), fold(slope)


def put_sums(sums_in, sums_ref, total, weight):
    for k in range(3):
        rows = slice(8 * k, 8 * k + 8)
        sums_ref[rows, :] = (sums_in[rows, :] if sums_in is not None else 0.0) + weight * total[k]


def unit_kernel(even_ref, image_ref, text_ref, a_ref, b_ref, parity_ref, slots, sems):
    parity_ref[...] = jnp.full(parity_ref.shape, even_ref[0], jnp.int32).astype(F32)
    even = even_ref[0] == 1
    parts = pieces(a_ref.shape[0])

    @pl.when(even)
    def _():
        for k, ref in enumerate((image_ref, text_ref)):
            for c, rows in enumerate(parts):
                pltpu.make_async_copy(ref.at[0, rows], slots.at[k, c], sems.at[k, c]).start()

    @pl.when(jnp.logical_not(even))
    def _():
        for k, ref in enumerate((text_ref, image_ref)):
            for c, rows in enumerate(parts):
                pltpu.make_async_copy(ref.at[0, rows], slots.at[k, c], sems.at[k, c]).start()

    for k, out_ref in enumerate((a_ref, b_ref)):
        for c, rows in enumerate(parts):
            pltpu.make_async_copy(image_ref.at[0, rows], slots.at[k, c], sems.at[k, c]).wait()
            out_ref[rows, :] = unit_rows(slots[k, c].astype(F32))[0].astype(LOW)


def unit_blocks(even, image, text):
    _, rows, width = image.shape
    full = pltpu.VMEM((rows, width), LOW)
    count = rows // TILE
    return pl.pallas_call(
        unit_kernel,
        in_specs=[smem(), hbm(), hbm()],
        out_specs=[vmem()] * 3,
        out_shape=[full, full, pltpu.VMEM((3, 128), F32)],
        scratch_shapes=[
            pltpu.VMEM((2, count, TILE, width), LOW),
            pltpu.SemaphoreType.DMA((2, count)),
        ],
        compiler_params=params(6),
        cost_estimate=cost(rows * width * 8, rows * width * 12),
        name="unit_blocks",
    )(even, *far(image, text))


def own_kernel(scalar_ref, a_ref, b_ref, slope_ref, sums_ref):
    temper, bias = scalar_ref[0], scalar_ref[1]
    total = None
    for rows in pieces(a_ref.shape[0]):
        raw = dot_t(a_ref[rows, :], b_ref[...])
        logits = temper * raw + bias
        row = lax.broadcasted_iota(jnp.int32, raw.shape, 0) + rows.start
        diagonal = row == lax.broadcasted_iota(jnp.int32, raw.shape, 1)
        grown = jnp.exp(jnp.where(diagonal, -logits, logits))
        part = share(grown)
        slope = jnp.where(diagonal, -part, part)
        slope_ref[rows, :] = slope.astype(LOW)
        part = sums_of(grown, slope, raw)
        total = part if total is None else [p + q for p, q in zip(total, part)]
    put_sums(None, sums_ref, total, 1.0)


def own_slopes(scalars, a, b):
    rows, width = a.shape
    return pl.pallas_call(
        own_kernel,
        in_specs=[smem(), vmem(), vmem()],
        out_specs=[vmem(), vmem()],
        out_shape=[pltpu.VMEM((rows, rows), LOW), pltpu.VMEM((24, 128), F32)],
        compiler_params=params(),
        cost_estimate=cost(2 * rows * rows * width, rows * width * 6, 3 * rows * rows),
        name="own_slopes",
    )(scalars, *near(a, b))


def pair_slopes(temper, bias, x, y):
    raw = dot_t(x, y)
    grown = jnp.exp(temper * raw + bias)
    return raw, grown, share(grown)


def slopes_kernel(scalar_ref, x_ref, y_ref, sums_in, slope_ref, sums_ref, *, weight):
    total = None
    for rows in pieces(x_ref.shape[0]):
        raw, grown, slope = pair_slopes(scalar_ref[0], scalar_ref[1], x_ref[rows, :], y_ref[...])
        slope_ref[rows, :] = slope.astype(LOW)
        part = sums_of(grown, slope, raw)
        total = part if total is None else [p + q for p, q in zip(total, part)]
    put_sums(sums_in, sums_ref, total, weight)


def slopes(scalars, x, y, sums, weight):
    rows, width = x.shape
    other = y.shape[0]
    return pl.pallas_call(
        functools.partial(slopes_kernel, weight=weight),
        in_specs=[smem(), vmem(), vmem(), vmem()],
        out_specs=[vmem(), vmem()],
        out_shape=[pltpu.VMEM((rows, other), LOW), pltpu.VMEM((24, 128), F32)],
        compiler_params=params(),
        cost_estimate=cost(2 * rows * other * width, (rows + other) * width * 4, 3 * rows * other),
        name="slopes",
    )(scalars, *near(x, y, sums))


def late_kernel(even_ref, scalar_ref, x_ref, y_ref, w_ref, sums_in, slope_ref, sums_ref):
    temper, bias = scalar_ref[0], scalar_ref[1]
    total = None
    for rows in pieces(x_ref.shape[0]):
        raw, grown, slope = pair_slopes(temper, bias, x_ref[rows, :], y_ref[...])
        slope_ref[rows, :] = slope.astype(LOW)
        part = sums_of(grown, slope, raw)
        total = part if total is None else [p + q for p, q in zip(total, part)]
    put_sums(sums_in, sums_ref, total, 1.0)
    half = x_ref.shape[0] // 2

    def rest(left_ref, right):
        total = None
        for rows in pieces(left_ref.shape[0]):
            raw, grown, slope = pair_slopes(temper, bias, left_ref[rows, :], right)
            part = sums_of(grown, slope, raw)
            total = part if total is None else [p + q for p, q in zip(total, part)]
        put_sums(sums_ref, sums_ref, total, 1.0)

    @pl.when(even_ref[0] == 1)
    def _():
        rest(w_ref, y_ref[half:, :])

    @pl.when(even_ref[0] == 0)
    def _():
        rest(y_ref, w_ref[:half, :])


def late_slopes(even, scalars, x, y, w, sums):
    rows, width = x.shape
    return pl.pallas_call(
        late_kernel,
        in_specs=[smem(), smem()] + [vmem()] * 4,
        out_specs=[vmem(), vmem()],
        out_shape=[pltpu.VMEM((rows, rows), LOW), pltpu.VMEM((24, 128), F32)],
        compiler_params=params(),
        cost_estimate=cost(3 * rows * rows * width, rows * width * 8, 4 * rows * rows),
        name="late_slopes",
    )(even, scalars, *near(x, y, w, sums))


def start_kernel(own_ref, a_ref, b_ref, other_ref, e_ref, ga_ref, gb_ref):
    for rows in pieces(a_ref.shape[0]):
        ga_ref[rows, :] = dot(own_ref[rows, :], b_ref[...])
        term = lax.dot_general(
            own_ref[:, rows], a_ref[...], (((0,), (0,)), ((), ())), preferred_element_type=F32
        )
        gb_ref[rows, :] = term + dot(other_ref[rows, :], e_ref[...])


def start_grads(own, a, b, other, e):
    rows, width = a.shape
    grad = pltpu.VMEM((rows, width), F32)
    return pl.pallas_call(
        start_kernel,
        in_specs=[vmem()] * 5,
        out_specs=[vmem()] * 2,
        out_shape=[grad, grad],
        compiler_params=params(),
        cost_estimate=cost(6 * rows * rows * width, rows * width * 16),
        name="start_grads",
    )(*near(own, a, b, other, e))


def back(grad, raw):
    raw = raw.astype(F32)
    scale = lax.rsqrt(jnp.sum(raw * raw, axis=-1, keepdims=True) + 1e-06)
    along = jnp.sum(raw * grad, axis=-1, keepdims=True) * (scale * scale * scale)
    return grad * scale - raw * along


def start_raw(first, even_in, odd_in, slots, sems, parts):
    @pl.when(first)
    def _():
        for c, rows in enumerate(parts):
            pltpu.make_async_copy(even_in.at[0, rows], slots.at[c], sems.at[0, c]).start()

    @pl.when(jnp.logical_not(first))
    def _():
        for c, rows in enumerate(parts):
            pltpu.make_async_copy(odd_in.at[0, rows], slots.at[c], sems.at[0, c]).start()


def start_out(first, c, rows, even_out, odd_out, slots, sems):
    @pl.when(first)
    def _():
        pltpu.make_async_copy(slots.at[c], even_out.at[0, rows], sems.at[1, c]).start()

    @pl.when(jnp.logical_not(first))
    def _():
        pltpu.make_async_copy(slots.at[c], odd_out.at[0, rows], sems.at[1, c]).start()


def finish_rows(first, temper, parts, grad_of, even_in, odd_in, even_out, odd_out, raws, slots, sems):
    start_raw(first, even_in, odd_in, raws, sems, parts)
    grad = grad_of(parts[0])
    for c, rows in enumerate(parts):
        pltpu.make_async_copy(even_in.at[0, rows], raws.at[c], sems.at[0, c]).wait()
    for c, rows in enumerate(parts):
        following = grad_of(parts[c + 1]) if c + 1 < len(parts) else None
        slots[c] = back(temper * grad, raws[c])
        start_out(first, c, rows, even_out, odd_out, slots, sems)
        grad = following
    for c, rows in enumerate(parts):
        pltpu.make_async_copy(slots.at[c], even_out.at[0, rows], sems.at[1, c]).wait()


def finish_scratch(parts, width):
    count, size = len(parts), parts[0].stop - parts[0].start
    return [
        pltpu.VMEM((count, size, width), LOW),
        pltpu.VMEM((count, size, width), F32),
        pltpu.SemaphoreType.DMA((2, count)),
    ]


def b_kernel(
    even_ref, scalar_ref, image_ref, text_ref, s_ref, p_ref, g_ref,
    image_out, text_out, raws, slots, sems, *, parts,
):
    def grad_of(rows):
        return g_ref[rows, :] + dot(s_ref[rows, :], p_ref[...])

    finish_rows(
        even_ref[0] == 1, scalar_ref[0], parts, grad_of,
        text_ref, image_ref, text_out, image_out, raws, slots, sems,
    )


def finish_b(even, scalars, image, text, s, p, grad):
    rows, width = grad.shape
    out = pltpu.HBM((1, rows, width), F32)
    parts = pieces(rows)
    return pl.pallas_call(
        functools.partial(b_kernel, parts=parts),
        in_specs=[smem(), smem(), hbm(), hbm()] + [vmem()] * 3,
        out_specs=[hbm()] * 2,
        out_shape=[out, out],
        scratch_shapes=finish_scratch(parts, width),
        compiler_params=params(14),
        cost_estimate=cost(2 * rows * rows * width, rows * width * 14),
        name="finish_b",
    )(even, scalars, *far(image, text), *near(s, p, grad))


def a_kernel(
    even_ref, scalar_ref, image_ref, text_ref, a_ref, f_ref, q_ref, g_ref, _image, _text,
    image_out, text_out, raws, slots, sems, *, parts,
):
    def grad_of(rows):
        total = g_ref[rows, :]
        for y_ref in (f_ref, q_ref):
            slope = pair_slopes(scalar_ref[0], scalar_ref[1], a_ref[rows, :], y_ref[...])[2]
            total = total + dot(slope.astype(LOW), y_ref[...])
        return total

    finish_rows(
        even_ref[0] == 1, scalar_ref[0], parts, grad_of,
        image_ref, text_ref, image_out, text_out, raws, slots, sems,
    )


def finish_a(parts, even, scalars, image, text, a, f, q, grad, image_out, text_out):
    rows, width = grad.shape
    out = pltpu.HBM((1, rows, width), F32)
    return pl.pallas_call(
        functools.partial(a_kernel, parts=parts),
        in_specs=[smem(), smem(), hbm(), hbm()] + [vmem()] * 4 + [hbm()] * 2,
        out_specs=[hbm()] * 2,
        out_shape=[out, out],
        input_output_aliases={8: 0, 9: 1},
        scratch_shapes=finish_scratch(parts, width),
        compiler_params=params(14),
        cost_estimate=cost(4 * rows * rows * width, rows * width * 20),
        name="finish_a",
    )(even, scalars, *far(image, text), *near(a, f, q, grad), *far(image_out, text_out))


def partner(block):
    count = lax.axis_size("blk")
    return lax.ppermute(block, "blk", [(i, i ^ 1) for i in range(count)])


def outward(block):
    count = lax.axis_size("blk")
    return lax.ppermute(block, "blk", [(i, (i + (2 if i % 2 else -2)) % count) for i in range(count)])


def inward(block):
    count = lax.axis_size("blk")
    return lax.ppermute(block, "blk", [(i, (i + (1 if i % 2 else -1)) % count) for i in range(count)])


def core_bit():
    return lax.axis_size("rep")


def swap_cores(sums):
    total = lax.axis_size("blk") * lax.axis_size("rep")
    route = [(i, i ^ core_bit()) for i in range(total)]
    return sums + lax.ppermute(sums, ("blk", "rep"), route)


def hand_over(even, sums, turn, mask):
    total, bit = lax.axis_size("blk") * lax.axis_size("rep"), core_bit()
    across = [(i, i ^ bit ^ (mask if (i & bit != 0) == (turn % 2 == 1) else 0)) for i in range(total)]
    beside = [(i, i ^ bit) for i in range(total)]
    came = lax.ppermute(sums, ("blk", "rep"), beside)
    if mask:
        came = came + lax.ppermute(sums, ("blk", "rep"), across)
    kept = even if turn % 2 == 0 else 1.0 - even
    return sums * kept + came * (1.0 - kept)


def after(value, *others):
    return lax.optimization_barrier((value, *others))[0]


def body(image, text, log_temp, bias):
    _, rows, width = image.shape
    temper = jnp.exp(log_temp)
    scalars = jnp.concatenate([temper, bias])
    even = (lax.rem(lax.axis_index("blk"), 2) == 0).astype(jnp.int32).reshape(1)

    a, b, parity = unit_blocks(even, image, text)
    p = outward(a)
    e = partner(b)
    w = partner(a)

    s_own, sums = own_slopes(scalars, a, b)
    q = inward(e)
    s_e, sums = slopes(scalars, b, e, sums, 0.5)
    grad_a, grad_b = start_grads(after(s_own, sums), a, b, s_e, e)
    s_p, sums = late_slopes(even, scalars, b, after(p, grad_b), w, sums)
    small = swap_cores(jnp.sum(sums.reshape(3, 8, 128), axis=1))
    f = partner(after(p, small))
    outs = None
    for turn, mask in enumerate(MASKS):
        total = hand_over(parity, small, turn, mask)
        if turn == 0:
            outs = finish_b(after(even, small), scalars, image, text, s_p, p, grad_b)
            total = after(total, outs[0])
        elif turn in A_TURNS:
            mine = [pieces(rows)[c] for c in A_TURNS[turn]]
            outs = finish_a(mine, after(even, small), scalars, image, text, a, f, q, grad_a, *outs)
            total = after(total, outs[0])
        small = total
        if turn == Q_TURN:
            small = after(small, q)
        if turn == F_TURN:
            small = after(small, f)
    small = hand_over(parity, small, len(MASKS), 0)
    grad_image, grad_text = outs

    pairs = float(lax.axis_size("rep") * lax.axis_size("blk") * rows * SPANS * rows)
    small = jnp.sum(small, axis=1) / pairs
    return (small[0:1], grad_image, grad_text, small[1:2] * temper, small[2:3])


def solution(mesh):
    return jax.shard_map(
        body,
        mesh=mesh,
        in_specs=(P("rep", "blk", None), P("rep", "blk", None), P(), P()),
        out_specs=(P(), P("rep", "blk", None), P("rep", "blk", None), P(), P()),
        check_vma=False,
    )
```

```python
import functools

import jax
import jax.numpy as jnp
from jax import lax
from jax.experimental import pallas as pl
from jax.experimental.pallas import tpu as pltpu
from jax.sharding import PartitionSpec as P

SPANS = 3
TILE = 256
LOW = jnp.bfloat16
F32 = jnp.float32
MASKS = (32, 1, 4, 128, 64, 16, 8)
Q_TURN, A_TURN = 2, 3


def params(mib=4):
    return pltpu.CompilerParams(vmem_limit_bytes=mib * 1024 * 1024)


def cost(flops, moved, trans=0):
    return pl.CostEstimate(flops=0, bytes_accessed=0, transcendentals=0)


def smem():
    return pl.BlockSpec(memory_space=pltpu.SMEM)


def vmem():
    return pl.BlockSpec(memory_space=pltpu.VMEM)


def hbm():
    return pl.BlockSpec(memory_space=pltpu.HBM)


def near(*values):
    return [pltpu.with_memory_space_constraint(v, pltpu.VMEM) for v in values]


def far(*values):
    return [pltpu.with_memory_space_constraint(v, pltpu.HBM) for v in values]


def unit_rows(raw):
    scale = lax.rsqrt(jnp.sum(raw * raw, axis=-1, keepdims=True) + 1e-06)
    return raw * scale, scale


def dot_t(x, y):
    return lax.dot_general(x, y, (((1,), (1,)), ((), ())), preferred_element_type=F32)


def dot(x, y):
    return jnp.dot(x, y, preferred_element_type=F32)


def pieces(rows, size=TILE):
    return [slice(r, r + size) for r in range(0, rows, size)]


def fold(values):
    rows, width = values.shape
    part = jnp.sum(values.reshape(rows // 8, 8, width), axis=0)
    return functools.reduce(jnp.add, [part[:, c : c + 128] for c in range(0, width, 128)])


def joined(p, q):
    return p + q + p * q


def log_fold(grown):
    rows, width = grown.shape
    groups = grown.reshape(rows // 64, 8, 8, width)
    parts = [groups[:, i] for i in range(8)]
    while len(parts) > 1:
        parts = [joined(p, q) for p, q in zip(parts[::2], parts[1::2])]
    return fold(jnp.log1p(parts[0]).reshape(rows // 8, width))


def share(grown):
    whole = 1.0 + grown
    inverse = pl.reciprocal(whole, approx=True)
    inverse = inverse * (2.0 - whole * inverse)
    return grown * inverse


def sums_of(grown, slope, raw):
    return log_fold(grown), fold(slope * raw), fold(slope)


def put_sums(sums_in, sums_ref, total, weight):
    for k in range(3):
        rows = slice(8 * k, 8 * k + 8)
        sums_ref[rows, :] = (sums_in[rows, :] if sums_in is not None else 0.0) + weight * total[k]


def unit_kernel(even_ref, image_ref, text_ref, a_ref, b_ref, parity_ref, slots, sems):
    parity_ref[...] = jnp.full(parity_ref.shape, even_ref[0], jnp.int32).astype(F32)
    even = even_ref[0] == 1
    parts = pieces(a_ref.shape[0])

    @pl.when(even)
    def _():
        for k, ref in enumerate((image_ref, text_ref)):
            for c, rows in enumerate(parts):
                pltpu.make_async_copy(ref.at[0, rows], slots.at[k, c], sems.at[k, c]).start()

    @pl.when(jnp.logical_not(even))
    def _():
        for k, ref in enumerate((text_ref, image_ref)):
            for c, rows in enumerate(parts):
                pltpu.make_async_copy(ref.at[0, rows], slots.at[k, c], sems.at[k, c]).start()

    for k, out_ref in enumerate((a_ref, b_ref)):
        for c, rows in enumerate(parts):
            pltpu.make_async_copy(image_ref.at[0, rows], slots.at[k, c], sems.at[k, c]).wait()
            out_ref[rows, :] = unit_rows(slots[k, c].astype(F32))[0].astype(LOW)


def unit_blocks(even, image, text):
    _, rows, width = image.shape
    full = pltpu.VMEM((rows, width), LOW)
    count = rows // TILE
    return pl.pallas_call(
        unit_kernel,
        in_specs=[smem(), hbm(), hbm()],
        out_specs=[vmem()] * 3,
        out_shape=[full, full, pltpu.VMEM((3, 128), F32)],
        scratch_shapes=[
            pltpu.VMEM((2, count, TILE, width), LOW),
            pltpu.SemaphoreType.DMA((2, count)),
        ],
        compiler_params=params(6),
        cost_estimate=cost(rows * width * 8, rows * width * 12),
        name="unit_blocks",
    )(even, *far(image, text))


def own_kernel(scalar_ref, a_ref, b_ref, slope_ref, sums_ref):
    temper, bias = scalar_ref[0], scalar_ref[1]
    total = None
    for rows in pieces(a_ref.shape[0]):
        raw = dot_t(a_ref[rows, :], b_ref[...])
        logits = temper * raw + bias
        row = lax.broadcasted_iota(jnp.int32, raw.shape, 0) + rows.start
        diagonal = row == lax.broadcasted_iota(jnp.int32, raw.shape, 1)
        grown = jnp.exp(jnp.where(diagonal, -logits, logits))
        part = share(grown)
        slope = jnp.where(diagonal, -part, part)
        slope_ref[rows, :] = slope.astype(LOW)
        part = sums_of(grown, slope, raw)
        total = part if total is None else [p + q for p, q in zip(total, part)]
    put_sums(None, sums_ref, total, 1.0)


def own_slopes(scalars, a, b):
    rows, width = a.shape
    return pl.pallas_call(
        own_kernel,
        in_specs=[smem(), vmem(), vmem()],
        out_specs=[vmem(), vmem()],
        out_shape=[pltpu.VMEM((rows, rows), LOW), pltpu.VMEM((24, 128), F32)],
        compiler_params=params(),
        cost_estimate=cost(2 * rows * rows * width, rows * width * 6, 3 * rows * rows),
        name="own_slopes",
    )(scalars, *near(a, b))


def pair_slopes(temper, bias, x, y):
    raw = dot_t(x, y)
    grown = jnp.exp(temper * raw + bias)
    return raw, grown, share(grown)


def slopes_kernel(scalar_ref, x_ref, y_ref, sums_in, slope_ref, sums_ref, *, weight):
    total = None
    for rows in pieces(x_ref.shape[0]):
        raw, grown, slope = pair_slopes(scalar_ref[0], scalar_ref[1], x_ref[rows, :], y_ref[...])
        slope_ref[rows, :] = slope.astype(LOW)
        part = sums_of(grown, slope, raw)
        total = part if total is None else [p + q for p, q in zip(total, part)]
    put_sums(sums_in, sums_ref, total, weight)


def slopes(scalars, x, y, sums, weight):
    rows, width = x.shape
    other = y.shape[0]
    return pl.pallas_call(
        functools.partial(slopes_kernel, weight=weight),
        in_specs=[smem(), vmem(), vmem(), vmem()],
        out_specs=[vmem(), vmem()],
        out_shape=[pltpu.VMEM((rows, other), LOW), pltpu.VMEM((24, 128), F32)],
        compiler_params=params(),
        cost_estimate=cost(2 * rows * other * width, (rows + other) * width * 4, 3 * rows * other),
        name="slopes",
    )(scalars, *near(x, y, sums))


def late_kernel(even_ref, scalar_ref, x_ref, y_ref, w_ref, sums_in, slope_ref, sums_ref):
    temper, bias = scalar_ref[0], scalar_ref[1]
    total = None
    for rows in pieces(x_ref.shape[0]):
        raw, grown, slope = pair_slopes(temper, bias, x_ref[rows, :], y_ref[...])
        slope_ref[rows, :] = slope.astype(LOW)
        part = sums_of(grown, slope, raw)
        total = part if total is None else [p + q for p, q in zip(total, part)]
    put_sums(sums_in, sums_ref, total, 1.0)
    half = x_ref.shape[0] // 2

    def rest(left_ref, right):
        total = None
        for rows in pieces(left_ref.shape[0]):
            raw, grown, slope = pair_slopes(temper, bias, left_ref[rows, :], right)
            part = sums_of(grown, slope, raw)
            total = part if total is None else [p + q for p, q in zip(total, part)]
        put_sums(sums_ref, sums_ref, total, 1.0)

    @pl.when(even_ref[0] == 1)
    def _():
        rest(w_ref, y_ref[half:, :])

    @pl.when(even_ref[0] == 0)
    def _():
        rest(y_ref, w_ref[:half, :])


def late_slopes(even, scalars, x, y, w, sums):
    rows, width = x.shape
    return pl.pallas_call(
        late_kernel,
        in_specs=[smem(), smem()] + [vmem()] * 4,
        out_specs=[vmem(), vmem()],
        out_shape=[pltpu.VMEM((rows, rows), LOW), pltpu.VMEM((24, 128), F32)],
        compiler_params=params(),
        cost_estimate=cost(3 * rows * rows * width, rows * width * 8, 4 * rows * rows),
        name="late_slopes",
    )(even, scalars, *near(x, y, w, sums))


def start_kernel(own_ref, a_ref, b_ref, other_ref, e_ref, ga_ref, gb_ref):
    for rows in pieces(a_ref.shape[0]):
        ga_ref[rows, :] = dot(own_ref[rows, :], b_ref[...])
        term = lax.dot_general(
            own_ref[:, rows], a_ref[...], (((0,), (0,)), ((), ())), preferred_element_type=F32
        )
        gb_ref[rows, :] = term + dot(other_ref[rows, :], e_ref[...])


def start_grads(own, a, b, other, e):
    rows, width = a.shape
    grad = pltpu.VMEM((rows, width), F32)
    return pl.pallas_call(
        start_kernel,
        in_specs=[vmem()] * 5,
        out_specs=[vmem()] * 2,
        out_shape=[grad, grad],
        compiler_params=params(),
        cost_estimate=cost(6 * rows * rows * width, rows * width * 16),
        name="start_grads",
    )(*near(own, a, b, other, e))


def back(grad, raw):
    raw = raw.astype(F32)
    scale = lax.rsqrt(jnp.sum(raw * raw, axis=-1, keepdims=True) + 1e-06)
    along = jnp.sum(raw * grad, axis=-1, keepdims=True) * (scale * scale * scale)
    return grad * scale - raw * along


def start_raw(first, even_in, odd_in, slots, sems, parts):
    @pl.when(first)
    def _():
        for c, rows in enumerate(parts):
            pltpu.make_async_copy(even_in.at[0, rows], slots.at[c], sems.at[0, c]).start()

    @pl.when(jnp.logical_not(first))
    def _():
        for c, rows in enumerate(parts):
            pltpu.make_async_copy(odd_in.at[0, rows], slots.at[c], sems.at[0, c]).start()


def start_out(first, c, rows, even_out, odd_out, slots, sems):
    @pl.when(first)
    def _():
        pltpu.make_async_copy(slots.at[c], even_out.at[0, rows], sems.at[1, c]).start()

    @pl.when(jnp.logical_not(first))
    def _():
        pltpu.make_async_copy(slots.at[c], odd_out.at[0, rows], sems.at[1, c]).start()


def finish_rows(first, temper, parts, grad_of, even_in, odd_in, even_out, odd_out, raws, slots, sems):
    start_raw(first, even_in, odd_in, raws, sems, parts)
    grad = grad_of(parts[0])
    for c, rows in enumerate(parts):
        pltpu.make_async_copy(even_in.at[0, rows], raws.at[c], sems.at[0, c]).wait()
    for c, rows in enumerate(parts):
        following = grad_of(parts[c + 1]) if c + 1 < len(parts) else None
        slots[c] = back(temper * grad, raws[c])
        start_out(first, c, rows, even_out, odd_out, slots, sems)
        grad = following
    for c, rows in enumerate(parts):
        pltpu.make_async_copy(slots.at[c], even_out.at[0, rows], sems.at[1, c]).wait()


def finish_scratch(parts, width):
    count, size = len(parts), parts[0].stop - parts[0].start
    return [
        pltpu.VMEM((count, size, width), LOW),
        pltpu.VMEM((count, size, width), F32),
        pltpu.SemaphoreType.DMA((2, count)),
    ]


def b_kernel(
    even_ref, scalar_ref, image_ref, text_ref, s_ref, p_ref, g_ref,
    image_out, text_out, raws, slots, sems, *, parts,
):
    def grad_of(rows):
        return g_ref[rows, :] + dot(s_ref[rows, :], p_ref[...])

    finish_rows(
        even_ref[0] == 1, scalar_ref[0], parts, grad_of,
        text_ref, image_ref, text_out, image_out, raws, slots, sems,
    )


def finish_b(even, scalars, image, text, s, p, grad):
    rows, width = grad.shape
    out = pltpu.HBM((1, rows, width), F32)
    parts = pieces(rows)
    return pl.pallas_call(
        functools.partial(b_kernel, parts=parts),
        in_specs=[smem(), smem(), hbm(), hbm()] + [vmem()] * 3,
        out_specs=[hbm()] * 2,
        out_shape=[out, out],
        scratch_shapes=finish_scratch(parts, width),
        compiler_params=params(14),
        cost_estimate=cost(2 * rows * rows * width, rows * width * 14),
        name="finish_b",
    )(even, scalars, *far(image, text), *near(s, p, grad))


def a_kernel(
    even_ref, scalar_ref, image_ref, text_ref, a_ref, f_ref, q_ref, g_ref, _image, _text,
    image_out, text_out, raws, slots, sems, *, parts,
):
    def grad_of(rows):
        total = g_ref[rows, :]
        for y_ref in (f_ref, q_ref):
            slope = pair_slopes(scalar_ref[0], scalar_ref[1], a_ref[rows, :], y_ref[...])[2]
            total = total + dot(slope.astype(LOW), y_ref[...])
        return total

    finish_rows(
        even_ref[0] == 1, scalar_ref[0], parts, grad_of,
        image_ref, text_ref, image_out, text_out, raws, slots, sems,
    )


def finish_a(even, scalars, image, text, a, f, q, grad, image_out, text_out):
    rows, width = grad.shape
    parts = pieces(rows)
    out = pltpu.HBM((1, rows, width), F32)
    return pl.pallas_call(
        functools.partial(a_kernel, parts=parts),
        in_specs=[smem(), smem(), hbm(), hbm()] + [vmem()] * 4 + [hbm()] * 2,
        out_specs=[hbm()] * 2,
        out_shape=[out, out],
        input_output_aliases={8: 0, 9: 1},
        scratch_shapes=finish_scratch(parts, width),
        compiler_params=params(14),
        cost_estimate=cost(4 * rows * rows * width, rows * width * 20),
        name="finish_a",
    )(even, scalars, *far(image, text), *near(a, f, q, grad), *far(image_out, text_out))


def partner(block):
    count = lax.axis_size("blk")
    return lax.ppermute(block, "blk", [(i, i ^ 1) for i in range(count)])


def outward(block):
    count = lax.axis_size("blk")
    return lax.ppermute(block, "blk", [(i, (i + (2 if i % 2 else -2)) % count) for i in range(count)])


def inward(block):
    count = lax.axis_size("blk")
    return lax.ppermute(block, "blk", [(i, (i + (1 if i % 2 else -1)) % count) for i in range(count)])


def core_bit():
    return lax.axis_size("rep")


def swap_cores(sums):
    total = lax.axis_size("blk") * lax.axis_size("rep")
    route = [(i, i ^ core_bit()) for i in range(total)]
    return sums + lax.ppermute(sums, ("blk", "rep"), route)


def hand_over(even, sums, turn, mask):
    total, bit = lax.axis_size("blk") * lax.axis_size("rep"), core_bit()
    across = [(i, i ^ bit ^ (mask if (i & bit != 0) == (turn % 2 == 1) else 0)) for i in range(total)]
    beside = [(i, i ^ bit) for i in range(total)]
    came = lax.ppermute(sums, ("blk", "rep"), beside)
    if mask:
        came = came + lax.ppermute(sums, ("blk", "rep"), across)
    kept = even if turn % 2 == 0 else 1.0 - even
    return sums * kept + came * (1.0 - kept)


def after(value, *others):
    return lax.optimization_barrier((value, *others))[0]


def body(image, text, log_temp, bias):
    _, rows, width = image.shape
    temper = jnp.exp(log_temp)
    scalars = jnp.concatenate([temper, bias])
    even = (lax.rem(lax.axis_index("blk"), 2) == 0).astype(jnp.int32).reshape(1)

    a, b, parity = unit_blocks(even, image, text)
    p = outward(a)
    e = partner(b)
    w = partner(a)

    s_own, sums = own_slopes(scalars, a, b)
    q = inward(e)
    s_e, sums = slopes(scalars, b, e, sums, 0.5)
    grad_a, grad_b = start_grads(after(s_own, sums), a, b, s_e, e)
    s_p, sums = late_slopes(even, scalars, b, after(p, grad_b), w, sums)
    small = swap_cores(jnp.sum(sums.reshape(3, 8, 128), axis=1))
    f = partner(after(p, small))
    outs = None
    for turn, mask in enumerate(MASKS):
        total = hand_over(parity, small, turn, mask)
        if turn == 0:
            outs = finish_b(after(even, small), scalars, image, text, s_p, p, grad_b)
            total = after(total, outs[0])
        elif turn == A_TURN:
            outs = finish_a(after(even, small), scalars, image, text, a, f, q, grad_a, *outs)
            total = after(total, outs[0])
        small = total
        if turn == Q_TURN:
            small = after(small, q)
    small = hand_over(parity, small, len(MASKS), 0)
    grad_image, grad_text = outs

    pairs = float(lax.axis_size("rep") * lax.axis_size("blk") * rows * SPANS * rows)
    small = jnp.sum(small, axis=1) / pairs
    return (small[0:1], grad_image, grad_text, small[1:2] * temper, small[2:3])


def solution(mesh):
    return jax.shard_map(
        body,
        mesh=mesh,
        in_specs=(P("rep", "blk", None), P("rep", "blk", None), P(), P()),
        out_specs=(P(), P("rep", "blk", None), P("rep", "blk", None), P(), P()),
        check_vma=False,
    )
```
